32 devices in a mesh: row: 8 (over z, core), col: 4 (over y, x).
Axes of the slice: x: 2, y: 2, z: 4, core: 2. Of those that a mesh axis runs over, the one named last changes fastest.
Arguments:
- genotypes: bfloat16 [5120, 16384], P(None, ('row', 'col')), may hold values from -5 to 5
- running: float32 [16384, 8, 4, 512], P('row', None, 'col'), as said below
- grid_map: int32 [8], replicated, may hold values from 0 to 7, each once
Outputs:
- factored: float32 [8, 8, 256, 8, 4, 512], P(None, 'row', None, None, 'col')
The draws below stay inside these ranges and needn't reach their ends.
Inputs may be any that keep to these rules, and one draw needn't show every extreme that they name: running is symmetric, and in its first 128 rows each diagonal entry exceeds the sum of the magnitudes of the row's other entries among the first 128 columns. grid_map holds each of its values once.
All inputs are finite; a program needn't handle non-finite values.
Results may differ from the reference program's by a relative error of at most 0.0003.
Values may be sent and summed in bfloat16 or wider, within the bound.
A program may use at most 256 MiB of HBM per device.

```python
import jax
import jax.numpy as jnp
from jax import lax

N = 16384
M = 5120
NB = 128
SHARD = 512
SUB = 256
N_ROW = 8
N_COL = 4


def draw_genotypes(key, part):
    first_key = jax.random.fold_in(jax.random.fold_in(key, 17), 0)
    values = jax.random.normal(first_key, (M, N), jnp.float32)
    return jnp.clip(values, -5.0, 5.0).astype(jnp.bfloat16)


def draw_running(key, part):
    first_key = jax.random.fold_in(key, 0)
    third_key = jax.random.fold_in(key, 2)
    noise = jax.random.uniform(first_key, (N, N), jnp.float32, -0.01, 0.01)
    index = jnp.arange(N)
    symmetric = jnp.where(index[:, None] <= index[None, :], noise, noise.T)
    diagonal = jax.random.uniform(third_key, (N,), jnp.float32, 2.0, 3.0)
    symmetric = jnp.where(index[:, None] == index[None, :], diagonal[:, None], symmetric)
    return symmetric.reshape(N, N_ROW, N_COL, N // (N_ROW * N_COL))


def setup_inputs(seed: int = 0) -> dict:
    arg_keys = jax.random.split(jax.random.key(seed), 4)
    genotypes = draw_genotypes(jax.random.fold_in(arg_keys[3], 71), 0)
    running = draw_running(jax.random.fold_in(arg_keys[3], 71), 0)
    grid_map = jax.random.permutation(arg_keys[2], N_ROW).astype(jnp.int32)
    return dict(genotypes=genotypes, running=running, grid_map=grid_map)


def reference(genotypes, running, grid_map):
    values = genotypes.astype(jnp.float32)
    product = jnp.dot(values.T, values, precision=lax.Precision.HIGHEST)
    updated = running.reshape(N, N) + product * (1.0 / M)
    lower = jnp.linalg.cholesky(updated[:NB, :NB])
    factor = lax.linalg.triangular_solve(lower, updated[:, :NB], left_side=False, lower=True, transpose_a=True)
    trail = updated - jnp.dot(factor, factor.T, precision=lax.Precision.HIGHEST)
    row_pos = jnp.arange(N, dtype=jnp.int32)[:, None]
    col_pos = jnp.arange(NB, dtype=jnp.int32)[None, :]
    left_part = jnp.where(row_pos >= col_pos, factor, jnp.zeros_like(factor))
    right_part = jnp.where(row_pos < NB, jnp.zeros_like(trail[:, NB:]), trail[:, NB:])
    finished = jnp.concatenate([left_part, right_part], axis=1)
    tiles = finished.reshape(N_ROW, N_ROW, SUB, N_ROW, N_COL, SHARD)
    inverse_map = jnp.argsort(grid_map).astype(jnp.int32)
    return jnp.take(tiles, inverse_map, axis=1)
```

```python
import functools
import math

import jax
import jax.numpy as jnp
from jax import lax
from jax.experimental import pallas as pl
from jax.experimental.pallas import tpu as pltpu
from jax.sharding import PartitionSpec as P

NB = 128
LANES = 128
OCTAVES = 24
STEPS = 32766.0 / OCTAVES
TINY = 1.1754944e-38
HUGE = 3.4028235e38


def shift_perm(n, s):
    return [(i, (i + s) % n) for i in range(n)]


def gather_shifts(x, axis):
    n = lax.axis_size(axis)
    me = lax.axis_index(axis)
    parts = [x] + [lax.ppermute(x, axis, shift_perm(n, s)) for s in range(1, n)]
    order = lax.rem(me - jnp.arange(n, dtype=jnp.int32) + n, n)
    return jnp.take(jnp.stack(parts), order, axis=0)


def broadcast_first(x, axis):
    n = lax.axis_size(axis)
    me = lax.axis_index(axis)
    have = 1
    while have < n:
        count = min(have, n - have)
        got = lax.ppermute(x, axis, [(i, i + have) for i in range(count)])
        x = jnp.where(me < have, x, got)
        have += count
    return x


def split_bf16(x):
    hi = x.astype(jnp.bfloat16)
    lo = (x - hi.astype(jnp.float32)).astype(jnp.bfloat16)
    return hi, lo


def finish_kernel(where_ref, a_ref, b_ref, run_ref, fa_ref, fb_ref, fac_ref, code_ref, scale_ref,
                  *, first, parts, shard, sub, tile, inv_m, block_rows):
    i = pl.program_id(0)
    row0 = where_ref[0] * block_rows + i * tile
    first_col = where_ref[1] == 0
    chunks = shard // LANES
    grow = row0 + lax.broadcasted_iota(jnp.int32, (tile, LANES), 0)
    cpos = lax.broadcasted_iota(jnp.int32, (tile, LANES), 1)
    top = grow < NB
    run = run_ref.reshape(tile * parts * chunks, LANES)
    for p in range(parts):
        acc = jnp.dot(a_ref[...], b_ref[p], preferred_element_type=jnp.float32) * inv_m
        acc = acc - jnp.dot(fa_ref[...], fb_ref[p], preferred_element_type=jnp.float32)
        pieces = []
        for j in range(chunks):
            g0 = run[pl.ds(p * chunks + j, tile, stride=parts * chunks), :]
            v = acc[:, j * LANES:(j + 1) * LANES] + g0
            v = jnp.where(top, 0.0, v)
            if first and p == 0 and j == 0:
                panel = jnp.where(grow >= cpos, fac_ref[...], 0.0)
                v = jnp.where(first_col, panel, v)
            pieces.append(v)
        for t in range(tile // sub):
            rows = slice(t * sub, (t + 1) * sub)
            mags = [jnp.abs(v[rows]) for v in pieces]
            peak = functools.reduce(jnp.maximum, mags)
            peak = jnp.max(peak, axis=0, keepdims=True)
            peak = jnp.max(peak, axis=1, keepdims=True)
            top_log = jnp.log2(jnp.maximum(jnp.broadcast_to(peak, (8, LANES)), TINY))
            scale_ref[t, p:p + 1, :] = top_log[:1]
            off = (OCTAVES - top_log[:1]) * STEPS + 1.5
            for j in range(chunks):
                v = pieces[j][rows]
                code = jnp.log2(jnp.maximum(mags[j], TINY)) * STEPS + off
                code = jnp.where(mags[j] > 0.0, jnp.maximum(code, 0.0), 0.0)
                code = jnp.minimum(code, 32767.0).astype(jnp.int32)
                code = jnp.where(v < 0.0, -code, code)
                col = (p * chunks + j) * LANES
                code_ref[t * sub:(t + 1) * sub, col:col + LANES] = code.astype(jnp.int16)


def decode_kernel(at_ref, *refs, parts, shard, sub):
    code_ref, scale_ref = refs[:2]
    out_ref = refs[-1]
    chunks = shard // LANES
    out = out_ref.reshape(sub * parts * chunks, LANES)
    for p in range(parts):
        base = scale_ref[0, p:p + 1, :] - OCTAVES - 1.0 / STEPS
        for j in range(chunks):
            col = (p * chunks + j) * LANES
            code = code_ref[:, col:col + LANES].astype(jnp.int32)
            mag = jnp.abs(code).astype(jnp.float32)
            v = jnp.minimum(jnp.exp2(mag * (1.0 / STEPS) + base), HUGE)
            v = jnp.where(code == 0, 0.0, jnp.where(code < 0, -v, v))
            out[pl.ds(p * chunks + j, sub, stride=parts * chunks), :] = v


def on_device(genotypes, running, grid_map):
    rows_count = lax.axis_size("row")
    cols_count = lax.axis_size("col")
    row_index = lax.axis_index("row")
    col_index = lax.axis_index("col")
    snp_count, shard = genotypes.shape
    block_rows = running.shape[0]
    sub = block_rows // rows_count
    p_count = running.shape[1]
    chunks = shard // LANES
    lanes_count = p_count * chunks
    inv_m = 1.0 / snp_count
    halves = 2
    parts = p_count // halves
    tile = sub * max(1, 512 // sub)
    tile = math.gcd(tile, block_rows)

    cols = lax.all_gather(genotypes, "row", axis=0)

    lead = broadcast_first(broadcast_first(genotypes[:, :NB], "row"), "col")
    run_panel = broadcast_first(running[:, 0, 0, :NB], "col")
    run_lead = broadcast_first(run_panel[:NB], "row")
    dims = (((0,), (0,)), ((), ()))
    lead_block = run_lead + lax.dot_general(lead, lead, dims, preferred_element_type=jnp.float32) * inv_m
    own_panel = lax.dynamic_slice_in_dim(run_panel, col_index * shard, shard, 0)
    own_panel = own_panel + lax.dot_general(
        genotypes, lead, dims, preferred_element_type=jnp.float32) * inv_m
    lower = jnp.linalg.cholesky(lead_block)
    own_factor = lax.linalg.triangular_solve(
        lower, own_panel, left_side=False, lower=True, transpose_a=True)
    row_factor = gather_shifts(own_factor, "col").reshape(block_rows, NB)
    col_factor = gather_shifts(own_factor, "row")
    hi, lo = split_bf16(row_factor)
    fa = jnp.concatenate([hi, hi, lo], axis=1)
    hi, lo = split_bf16(jnp.swapaxes(col_factor, 1, 2))
    fb = jnp.concatenate([hi, lo, hi], axis=1)

    mine_rows = gather_shifts(genotypes.T, "col").reshape(block_rows, snp_count)

    run = running.reshape(block_rows, lanes_count, LANES)
    where = jnp.stack([row_index, col_index]).astype(jnp.int32)
    inverse_map = jnp.argsort(grid_map).astype(jnp.int32)
    width = parts * shard
    vmem = 60 * 1024 * 1024

    out = None
    for h in range(halves):
        codes, scales = pl.pallas_call(
            functools.partial(finish_kernel, first=h == 0, parts=parts, shard=shard, sub=sub,
                              tile=tile, inv_m=inv_m, block_rows=block_rows),
            grid_spec=pltpu.PrefetchScalarGridSpec(
                num_scalar_prefetch=1,
                grid=(block_rows // tile,),
                in_specs=[
                    pl.BlockSpec((tile, snp_count), lambda i, w: (i, 0)),
                    pl.BlockSpec((parts, snp_count, shard), lambda i, w, h=h: (h, 0, 0),
                                 pipeline_mode=pl.Buffered(1)),
                    pl.BlockSpec((tile, parts * chunks, LANES), lambda i, w, h=h: (i, h, 0)),
                    pl.BlockSpec((tile, 3 * NB), lambda i, w: (i, 0)),
                    pl.BlockSpec((parts, 3 * NB, shard), lambda i, w, h=h: (h, 0, 0)),
                    pl.BlockSpec((tile, NB), lambda i, w: (i, 0)),
                ],
                out_specs=[
                    pl.BlockSpec((tile, width), lambda i, w: (i, 0)),
                    pl.BlockSpec((tile // sub, parts, LANES), lambda i, w: (i, 0, 0)),
                ],
            ),
            out_shape=[
                jax.ShapeDtypeStruct((block_rows, width), jnp.int16),
                jax.ShapeDtypeStruct((rows_count, parts, LANES), jnp.float32),
            ],
            compiler_params=pltpu.CompilerParams(vmem_limit_bytes=vmem),
            cost_estimate=pl.CostEstimate(
                flops=2 * block_rows * snp_count * width,
                bytes_accessed=2 * snp_count * (block_rows + width) + 6 * block_rows * width,
                transcendentals=block_rows * width),
            name=f"finish_{h}",
        )(where, mine_rows, cols, run, fa, fb, row_factor)
        for s in range(rows_count):
            target = lax.rem(row_index + s, rows_count)
            k = lax.dynamic_index_in_dim(inverse_map, target, 0, keepdims=False)
            part = lax.dynamic_slice_in_dim(codes, k * sub, sub, 0)
            scale = lax.dynamic_slice_in_dim(scales, k, 1, 0)
            if s:
                part = lax.ppermute(part, "row", shift_perm(rows_count, s))
                scale = lax.ppermute(scale, "row", shift_perm(rows_count, s))
            source = lax.rem(row_index - s + rows_count, rows_count).reshape(1)
            args = [source, part, scale]
            specs = [
                pl.BlockSpec((sub, width), lambda i, at: (0, 0)),
                pl.BlockSpec((1, parts, LANES), lambda i, at: (0, 0, 0)),
            ]
            if out is not None:
                args.append(out)
                specs.append(pl.BlockSpec(memory_space=pl.ANY))
            out = pl.pallas_call(
                functools.partial(decode_kernel, parts=parts, shard=shard, sub=sub),
                grid_spec=pltpu.PrefetchScalarGridSpec(
                    num_scalar_prefetch=1,
                    grid=(1,),
                    in_specs=specs,
                    out_specs=pl.BlockSpec((None, sub, parts * chunks, LANES),
                                           lambda i, at, h=h: (at[0], 0, h, 0)),
                ),
                out_shape=jax.ShapeDtypeStruct((rows_count, sub, lanes_count, LANES), jnp.float32),
                input_output_aliases={3: 0} if out is not None else {},
                compiler_params=pltpu.CompilerParams(vmem_limit_bytes=vmem),
                cost_estimate=pl.CostEstimate(
                    flops=10 * sub * width, bytes_accessed=6 * sub * width,
                    transcendentals=sub * width),
                name="decode",
            )(*args)
    return out.reshape(rows_count, 1, sub, p_count, 1, shard)


def solution(mesh):
    in_specs = (P(None, ("row", "col")), P("row", None, "col", None), P())
    out_specs = P(None, "row", None, None, "col", None)
    return jax.shard_map(
        on_device, mesh=mesh, in_specs=in_specs, out_specs=out_specs, check_vma=False
    )
```
